256 devices in a mesh: ctx: 32 (over z_lo, x, core), tp: 8 (over z_hi, y).
Axes of the slice: x: 4, y: 4, z: 8 (z_hi: 2, z_lo: 4; z = z_hi * 4 + z_lo), core: 2. Of those that a mesh axis runs over, the one named last changes fastest.
Arguments:
- tokens: bfloat16 [16384, 8192], P('ctx', 'tp'), may hold values from -6 to 6
- in_weight: bfloat16 [8192, 3, 1024], P('tp'), may hold values from -0.0625 to 0.0625
- skip_gain: float32 [1024], P('tp'), may hold values from 0.5 to 1.5
- response: float32 [2, 512, 64, 1024], P(None, None, 'ctx', 'tp'), may hold values from -6 to 6
Outputs:
- mixed: bfloat16 [16384, 1024], P('ctx', 'tp')
The draws below stay inside these ranges and needn't reach their ends.
All inputs are finite; a program needn't handle non-finite values.
Results may differ from the reference program's by a relative error of at most 0.027.
Values may be sent and summed in bfloat16 or wider, within the bound.
A program may use at most 64 MiB of HBM per device.

```python
import jax
import jax.numpy as jnp
import numpy as np
from jax import lax

D = 8192
CH = 1024
TOK_DEV = 512
TOKENS = 16384
N_CTX = 32
N_TP = 8


def block_levels(key, extent, pieces, smallest, high):
    level, own = 1.0, jax.random.fold_in(key, 6)
    for dim, shards_of in pieces:
        draws = jnp.exp(jax.random.uniform(jax.random.fold_in(own, dim), (shards_of,), jnp.float32, smallest / len(pieces), high / len(pieces)))
        level = level * jnp.repeat(draws, extent[dim] // shards_of).reshape([-1 if axis == dim else 1 for axis in range(len(extent))])
    return level


def centred(rng, shape, scale, bound, shards=(), kind=jnp.bfloat16):
    entries = scale * jax.random.normal(rng, shape, jnp.float32)
    if shards:
        entries = entries * block_levels(rng, shape, shards, -0.22, 0.18)
    return jnp.clip(entries, -bound, bound).astype(kind)


def setup_inputs(seed: int = 0) -> dict:
    key_list = jax.random.split(jax.random.key(seed), 5)
    tokens = centred(key_list[0], (TOKENS, D), 1.0, 6.0, ((0, 32), (1, 8)))
    in_weight = centred(key_list[1], (D, 3, CH), D ** -0.5, 0.0625, ((0, 8),))
    skip_gain = jnp.clip(0.5 + 1.0 * jax.random.uniform(key_list[2], (CH,), jnp.float32) ** block_levels(key_list[2], (CH,), ((0, 8),), -0.2, 0.2), 0.5, 1.5)
    response = centred(key_list[3], (2, TOK_DEV, 2 * N_CTX, CH), 1.0, 6.0, ((2, 32), (3, 8)), jnp.float32)
    return {"tokens": tokens, "in_weight": in_weight, "skip_gain": skip_gain, "response": response}


def frequency_order(devices):
    bit_count = devices.bit_length() - 1
    listing = []
    for position in range(2 * devices):
        pair_index = position // 2
        flipped = 0
        for level in range(bit_count):
            flipped = flipped * 2 + ((pair_index >> level) & 1)
        listing.append(2 * flipped + position % 2)
    return np.array(listing, dtype=np.int32)


def reference(tokens, in_weight, skip_gain, response):
    block_width = D // N_TP
    flat_weight = in_weight.reshape(D, 3 * CH)
    proj = jnp.zeros((TOKENS, 3 * CH), jnp.float32)
    for block in range(N_TP):
        partial_term = jnp.dot(tokens[:, block * block_width:(block + 1) * block_width],
                               flat_weight[block * block_width:(block + 1) * block_width],
                               preferred_element_type=jnp.float32)
        rounded = lax.optimization_barrier(partial_term.astype(jnp.bfloat16))
        proj = proj + rounded.astype(jnp.float32)
    proj = proj.reshape(TOKENS, 3, CH)
    query = proj[:, 0, :]
    gated = proj[:, 1, :] * proj[:, 2, :]
    padded = jnp.concatenate([gated, jnp.zeros_like(gated)], axis=0)
    spectrum = jnp.fft.fft(padded, axis=0).reshape(TOK_DEV, 2 * N_CTX, CH)
    listing = frequency_order(N_CTX)
    arranged = spectrum[:, listing, :]
    filtered = arranged * (response[0] + 1j * response[1])
    natural = filtered[:, listing, :].reshape(2 * TOKENS, CH)
    conv = jnp.real(jnp.fft.ifft(natural, axis=0))[:TOKENS]
    mixed = query * (conv + skip_gain * gated)
    return mixed.astype(jnp.bfloat16)
```

```python
import functools
import math

import jax
import jax.numpy as jnp
import numpy as np
from jax import lax
from jax.experimental import pallas as pl
from jax.experimental.pallas import tpu as pltpu
from jax.sharding import PartitionSpec as P

MESH = pl.DeviceIdType.MESH
F32 = jnp.float32
BF16 = jnp.bfloat16
UNITS = 6


def tables():
    row = np.arange(256)
    dev, inner = row // 8, row % 8
    rev = sum(((dev >> level) & 1) << (4 - level) for level in range(5))
    k1 = 2 * rev + inner % 2 + 64 * (inner // 2)
    col = np.arange(128)
    n1 = 4 * (col % 32) + col // 32
    n2 = np.arange(128)
    ang1 = 2 * np.pi / 256 * (k1[:, None] * n1[None, :] % 256)
    first = np.concatenate([np.cos(ang1), -np.sin(ang1)], axis=0)
    last = np.concatenate([np.cos(ang1).T, -np.sin(ang1).T], axis=1) / 32768
    ang2 = 2 * np.pi / 128 * (n2[:, None] * n2[None, :] % 128)
    c2, s2 = np.cos(ang2), np.sin(ang2)
    second = np.block([[c2, -s2], [s2, c2]])
    back = np.block([[c2, s2], [-s2, c2]])
    tw = 2 * np.pi / 32768 * (k1[:, None] * n2[None, :])
    bf = lambda a: jnp.asarray(a.astype(np.float32).astype(BF16))
    twist = jnp.asarray(np.stack([np.cos(tw), np.sin(tw)]).astype(np.float32))
    return bf(first), bf(second), bf(back), bf(last), twist


def kernel(tok_h, w_h, skip_ref, rsp_h, f1_h, f2_h, g2_h, g1_h, tw_h, o_ref,
           tok, w, rsp, f1, f2, g2, g1, tw,
           sa, ra, sb, rb, sc, rc, part, gat, query,
           hs32, hs, hr, g32, gs, gr, cs, cr,
           load_sem, sa_sem, ra_sem, sb_sem, rb_sem, sc_sem, rc_sem, x_send, x_recv):
    me = lax.axis_index("ctx")
    t = lax.axis_index("tp")
    zh, y = t // 4, t % 4
    up = (me, zh * 4 + (y + 1) % 4)
    down = (me, zh * 4 + (y + 3) % 4)
    across = (me, (1 - zh) * 4 + y)

    loads = [(tok_h, tok), (w_h.at[1], w.at[1]), (w_h.at[2], w.at[2]), (rsp_h, rsp), (w_h.at[0], w.at[0]),
             (f1_h, f1), (f2_h, f2), (g2_h, g2), (g1_h, g1), (tw_h, tw)]
    loads = [pltpu.make_async_copy(src, dst, load_sem.at[i]) for i, (src, dst) in enumerate(loads)]
    for copy in loads:
        copy.start()

    barrier = pltpu.get_barrier_semaphore()
    for dev in (up, down, across):
        pl.semaphore_signal(barrier, inc=1, device_id=dev, device_id_type=MESH)

    def greet(k, carry):
        pl.semaphore_signal(barrier, inc=1, device_id=((me + k) % 32, t), device_id_type=MESH)
        return carry

    lax.fori_loop(1, 32, greet, 0)

    def term(u, dest_y):
        rows = pl.ds(u % 2 * 256, 256)
        far = pl.ds(pl.multiple_of(((1 - zh) * 4 + dest_y) * 128, 128), 128)
        near = pl.ds(pl.multiple_of((zh * 4 + dest_y) * 128, 128), 128)
        if u < 2:
            rhs = [w[1, :, far], w[2, :, far]]
        elif u < 4:
            rhs = [w[1, :, near], w[2, :, near]]
        else:
            rhs = [w[0, :, far], w[0, :, near]]
        return jnp.dot(tok[rows, :], jnp.concatenate(rhs, axis=1), preferred_element_type=F32)

    def remote(src, dst, ssem, rsem, dev):
        return pltpu.make_async_remote_copy(src_ref=src, dst_ref=dst, send_sem=ssem, recv_sem=rsem,
                                            device_id=dev, device_id_type=MESH)

    lo, hi = pl.ds(0, 128), pl.ds(128, 128)

    def a_copy(u, side):
        part_rows = (lo, hi)[side]
        return remote(sa.at[u, part_rows], ra.at[u, part_rows], sa_sem.at[u, side], ra_sem.at[u, side], (up, down)[side])

    def b_copy(u, side, half):
        part_rows = (lo, hi)[half]
        return remote(sb.at[u, side, part_rows], rb.at[u, side, part_rows], sb_sem.at[u, 2 * side + half],
                      rb_sem.at[u, 2 * side + half], (up, down)[side])

    def c_copy(u):
        if u < 2:
            return remote(sc.at[u], rc.at[u], sc_sem.at[u], rc_sem.at[u], across)
        return remote(sc.at[u - 2, :, lo], rc.at[u - 2, :, lo], sc_sem.at[u - 2], rc_sem.at[u - 2], across)

    def compute_a(u):
        sa[u] = term(u, (y + 2) % 4).astype(BF16)

    def send_a(u):
        a_copy(u, 0).start()
        a_copy(u, 1).start()

    def raw(u):
        for side, step in ((0, 1), (1, 3)):
            value = term(u, (y + step) % 4)
            through, direct = (value[:128], value[128:]) if side == 0 else (value[128:], value[:128])
            sb[u, side, (hi, lo)[side], :] = direct.astype(BF16)
            b_copy(u, side, 1 - side).start()
            part[u % 2, side] = through

    def add(u):
        for side in (0, 1):
            a_copy(u, side).wait_recv()
            rows = (lo, hi)[side]
            sb[u, side, rows, :] = (part[u % 2, side] + ra[u, rows, :].astype(F32)).astype(BF16)
            b_copy(u, side, side).start()

    def finish(u):
        own = term(u, y)
        for side in (0, 1):
            for half in (0, 1):
                b_copy(u, side, half).wait_recv()
        total = own + rb[u, 0].astype(F32) + rb[u, 1].astype(F32)
        rows = pl.ds(u % 2 * 256, 256)
        if u < 2:
            sc[u] = total.astype(BF16)
            c_copy(u).start()
        elif u < 4:
            c_copy(u - 2).wait_recv()
            total = total + rc[u - 2].astype(F32)
            product = total[:, :128] * total[:, 128:]
            gat[rows, :] = product
            for half in (0, 1):
                s = u % 2 * 2 + half
                g32[pl.ds(s, 128, stride=4), :] = jnp.transpose(product[half * 128:half * 128 + 128, :])
        else:
            sc[u - 2, :, lo] = total[:, :128].astype(BF16)
            query[rows, :] = total[:, 128:]
            c_copy(u).start()

    def spread(src, dst, which):
        def go(k, carry):
            to = (me + k) % 32
            remote(src.at[to], dst.at[me], x_send.at[which], x_recv.at[which], (to, t)).start()
            return carry

        lax.fori_loop(1, 32, go, 0)
        dst[me] = src[me]

    def arrived(dst, which):
        others = dst.at[pl.ds(0, 31)]
        pltpu.make_async_copy(others, others, x_recv.at[which]).wait()

    def left(src, which):
        others = src.at[pl.ds(0, 31)]
        pltpu.make_async_copy(others, others, x_send.at[which]).wait()

    for i in range(3):
        loads[i].wait()
    compute_a(0)
    pl.semaphore_wait(barrier, 34)
    send_a(0)
    raw(0)
    compute_a(1)
    send_a(1)

    loads[3].wait()
    for ri in range(2):
        for b in range(8):
            hs32[pl.ds(ri * 8 + b, 128, stride=16), :] = jnp.transpose(rsp[ri, pl.ds(b, 128, stride=8), :])
    hs[...] = hs32[...].astype(BF16).reshape(32, 64, 128)
    spread(hs, hr, 0)

    add(0)
    raw(1)
    compute_a(2)
    send_a(2)
    add(1)
    finish(0)
    raw(2)
    compute_a(3)
    send_a(3)
    add(2)
    finish(1)
    raw(3)
    loads[4].wait()
    compute_a(4)
    send_a(4)
    add(3)
    finish(2)
    raw(4)
    finish(3)
    gs[...] = g32[...].astype(BF16).reshape(32, 16, 128)
    spread(gs, gr, 1)
    compute_a(5)
    send_a(5)
    add(4)
    raw(5)
    add(5)
    finish(4)
    for i in range(5, 10):
        loads[i].wait()
    arrived(hr, 0)
    arrived(gr, 1)

    g32[...] = gr[...].astype(F32).reshape(512, 128)
    signal = jnp.concatenate(
        [jnp.concatenate([g32[pl.ds(c * 4 + s, 32, stride=16), :] for s in range(4)], axis=0) for c in range(4)],
        axis=1).astype(BF16)
    mid = jnp.dot(f1[...], signal, preferred_element_type=F32)
    cosine, sine = tw[0], tw[1]
    columns = []
    for c in range(4):
        lanes = slice(c * 128, c * 128 + 128)
        re, im = mid[:256, lanes], mid[256:, lanes]
        turned = jnp.concatenate([re * cosine + im * sine, im * cosine - re * sine], axis=1).astype(BF16)
        spec = jnp.dot(turned, f2[...], preferred_element_type=F32)
        resp = hr[:, 16 * c:16 * c + 16, :].astype(F32)
        resp_re = resp[:, :8, :].reshape(256, 128)
        resp_im = resp[:, 8:, :].reshape(256, 128)
        re, im = spec[:, :128], spec[:, 128:]
        filtered = jnp.concatenate([re * resp_re - im * resp_im, re * resp_im + im * resp_re], axis=1).astype(BF16)
        back = jnp.dot(filtered, g2[...], preferred_element_type=F32)
        re, im = back[:, :128], back[:, 128:]
        columns.append(jnp.concatenate([re * cosine - im * sine, re * sine + im * cosine], axis=0).astype(BF16))
    conv = jnp.dot(g1[...], jnp.concatenate(columns, axis=1), preferred_element_type=F32)
    for c in range(4):
        for s in range(4):
            g32[pl.ds(c * 4 + s, 32, stride=16), :] = conv[s * 32:s * 32 + 32, c * 128:c * 128 + 128]
    cs[...] = g32[...].astype(BF16).reshape(32, 16, 128)
    spread(cs, cr, 2)

    finish(5)
    for u in (4, 5):
        c_copy(u).wait_recv()
    gain = skip_ref[...]
    arrived(cr, 2)
    g32[...] = cr[...].astype(F32).reshape(512, 128)
    for s in range(4):
        rows = pl.ds(s * 128, 128)
        conv_rows = jnp.transpose(g32[pl.ds(s, 128, stride=4), :])
        q = query[rows, :] + rc[2 + s // 2, pl.ds(s % 2 * 128, 128), lo].astype(F32)
        o_ref[rows, :] = (q * (conv_rows + gain * gat[rows, :])).astype(BF16)

    for u in range(UNITS):
        for side in (0, 1):
            a_copy(u, side).wait_send()
            for half in (0, 1):
                b_copy(u, side, half).wait_send()
    for u in (0, 1, 4, 5):
        c_copy(u).wait_send()
    for src, which in ((hs, 0), (gs, 1), (cs, 2)):
        left(src, which)


def per_device(tokens, in_weight, skip_gain, response):
    first, second, back, last, twist = tables()
    anywhere = pl.BlockSpec(memory_space=pltpu.HBM)
    vmem = pl.BlockSpec(memory_space=pltpu.VMEM)
    return pl.pallas_call(
        kernel,
        out_shape=jax.ShapeDtypeStruct((512, 128), BF16),
        in_specs=[anywhere, anywhere, vmem] + [anywhere] * 6,
        out_specs=vmem,
        scratch_shapes=[
            pltpu.VMEM((512, 1024), BF16),
            pltpu.VMEM((3, 1024, 1024), BF16),
            pltpu.VMEM((2, 1024, 128), F32),
            pltpu.VMEM((512, 128), BF16),
            pltpu.VMEM((256, 256), BF16),
            pltpu.VMEM((256, 256), BF16),
            pltpu.VMEM((128, 512), BF16),
            pltpu.VMEM((2, 256, 128), F32),
            pltpu.VMEM((UNITS, 256, 256), BF16),
            pltpu.VMEM((UNITS, 256, 256), BF16),
            pltpu.VMEM((UNITS, 2, 256, 256), BF16),
            pltpu.VMEM((UNITS, 2, 256, 256), BF16),
            pltpu.VMEM((4, 256, 256), BF16),
            pltpu.VMEM((4, 256, 256), BF16),
            pltpu.VMEM((2, 2, 128, 256), F32),
            pltpu.VMEM((512, 128), F32),
            pltpu.VMEM((512, 128), F32),
            pltpu.VMEM((2048, 128), F32),
            pltpu.VMEM((32, 64, 128), BF16),
            pltpu.VMEM((32, 64, 128), BF16),
            pltpu.VMEM((512, 128), F32),
            pltpu.VMEM((32, 16, 128), BF16),
            pltpu.VMEM((32, 16, 128), BF16),
            pltpu.VMEM((32, 16, 128), BF16),
            pltpu.VMEM((32, 16, 128), BF16),
            pltpu.SemaphoreType.DMA((10,)),
            pltpu.SemaphoreType.DMA((UNITS, 2)),
            pltpu.SemaphoreType.DMA((UNITS, 2)),
            pltpu.SemaphoreType.DMA((UNITS, 4)),
            pltpu.SemaphoreType.DMA((UNITS, 4)),
            pltpu.SemaphoreType.DMA((4,)),
            pltpu.SemaphoreType.DMA((4,)),
            pltpu.SemaphoreType.DMA((3,)),
            pltpu.SemaphoreType.DMA((3,)),
        ],
        compiler_params=pltpu.CompilerParams(
            collective_id=0, has_side_effects=True, vmem_limit_bytes=48 * 1024 * 1024
        ),
        cost_estimate=pl.CostEstimate(flops=4_000_000_000, bytes_accessed=9_000_000, transcendentals=0),
    )(tokens, jnp.transpose(in_weight, (1, 0, 2)), skip_gain.reshape(1, 128), response.reshape(2, 1024, 128),
      first, second, back, last, twist)


def solution(mesh):
    in_specs = (P("ctx", "tp"), P("tp", None, None), P("tp"), P(None, None, "ctx", "tp"))
    return jax.shard_map(
        per_device, mesh=mesh, in_specs=in_specs, out_specs=P("ctx", "tp"), check_vma=False
    )
```

```python
import functools
import math

import jax
import jax.numpy as jnp
import numpy as np
from jax import lax
from jax.experimental import pallas as pl
from jax.experimental.pallas import tpu as pltpu
from jax.sharding import PartitionSpec as P

MESH = pl.DeviceIdType.MESH
F32 = jnp.float32
BF16 = jnp.bfloat16
UNITS = 6


def tables():
    row = np.arange(256)
    dev, inner = row // 8, row % 8
    rev = sum(((dev >> level) & 1) << (4 - level) for level in range(5))
    k1 = 2 * rev + inner % 2 + 64 * (inner // 2)
    col = np.arange(128)
    n1 = 4 * (col % 32) + col // 32
    n2 = np.arange(128)
    ang1 = 2 * np.pi / 256 * (k1[:, None] * n1[None, :] % 256)
    first = np.concatenate([np.cos(ang1), -np.sin(ang1)], axis=0)
    last = np.concatenate([np.cos(ang1).T, -np.sin(ang1).T], axis=1) / 32768
    ang2 = 2 * np.pi / 128 * (n2[:, None] * n2[None, :] % 128)
    c2, s2 = np.cos(ang2), np.sin(ang2)
    second = np.block([[c2, -s2], [s2, c2]])
    back = np.block([[c2, s2], [-s2, c2]])
    tw = 2 * np.pi / 32768 * (k1[:, None] * n2[None, :])
    bf = lambda a: jnp.asarray(a.astype(np.float32).astype(BF16))
    twist = jnp.asarray(np.stack([np.cos(tw), np.sin(tw)]).astype(np.float32))
    return bf(first), bf(second), bf(back), bf(last), twist


def kernel(tok_h, w_h, skip_ref, rsp_h, f1_h, f2_h, g2_h, g1_h, tw_h, o_ref,
           tok, w, rsp, f1, f2, g2, g1, tw,
           sa, ra, sb, rb, sc, rc, part, gat, query,
           hs32, hs, hr, g32, gs, gr, cs, cr,
           load_sem, sa_sem, ra_sem, sb_sem, rb_sem, sc_sem, rc_sem, x_send, x_recv):
    me = lax.axis_index("ctx")
    t = lax.axis_index("tp")
    zh, y = t // 4, t % 4
    up = (me, zh * 4 + (y + 1) % 4)
    down = (me, zh * 4 + (y + 3) % 4)
    across = (me, (1 - zh) * 4 + y)

    def columns(z, dest_y):
        return pl.ds(pl.multiple_of((z * 4 + dest_y) * 128, 128), 128)

    far, near = 1 - zh, zh
    pieces = [(rsp_h, rsp), (tok_h, tok), (w_h.at[1], w.at[1]), (w_h.at[2], w.at[2]), (w_h.at[0], w.at[0]),
              (f1_h, f1), (f2_h, f2), (g2_h, g2), (g1_h, g1), (tw_h, tw)]
    loads = [pltpu.make_async_copy(src, dst, load_sem.at[i]) for i, (src, dst) in enumerate(pieces)]
    for copy in loads:
        copy.start()
    waited = []

    def need(count):
        while len(waited) < count:
            loads[len(waited)].wait()
            waited.append(True)

    barrier = pltpu.get_barrier_semaphore()
    for dev in (up, down, across):
        pl.semaphore_signal(barrier, inc=1, device_id=dev, device_id_type=MESH)

    def greet(k, carry):
        pl.semaphore_signal(barrier, inc=1, device_id=((me + k) % 32, t), device_id_type=MESH)
        return carry

    lax.fori_loop(1, 32, greet, 0)

    def term(u, dest_y):
        if u >= 4:
            value = jnp.dot(tok[...], w[0, :, columns((far, near)[u - 4], dest_y)], preferred_element_type=F32)
            return jnp.concatenate([value[:256], value[256:]], axis=1)
        rows = pl.ds(u % 2 * 256, 256)
        if u < 2:
            rhs = [w[1, :, columns(far, dest_y)], w[2, :, columns(far, dest_y)]]
        else:
            rhs = [w[1, :, columns(near, dest_y)], w[2, :, columns(near, dest_y)]]
        return jnp.dot(tok[rows, :], jnp.concatenate(rhs, axis=1), preferred_element_type=F32)

    def remote(src, dst, ssem, rsem, dev):
        return pltpu.make_async_remote_copy(src_ref=src, dst_ref=dst, send_sem=ssem, recv_sem=rsem,
                                            device_id=dev, device_id_type=MESH)

    lo, hi = pl.ds(0, 128), pl.ds(128, 128)

    def a_copy(u, side):
        part_rows = (lo, hi)[side]
        return remote(sa.at[u, part_rows], ra.at[u, part_rows], sa_sem.at[u, side], ra_sem.at[u, side], (up, down)[side])

    def b_copy(u, side, half):
        part_rows = (lo, hi)[half]
        return remote(sb.at[u, side, part_rows], rb.at[u, side, part_rows], sb_sem.at[u, 2 * side + half],
                      rb_sem.at[u, 2 * side + half], (up, down)[side])

    def c_copy(u):
        slot = min(u, 2)
        return remote(sc.at[slot], rc.at[slot], sc_sem.at[slot], rc_sem.at[slot], across)

    def compute_a(u):
        sa[u] = term(u, (y + 2) % 4).astype(BF16)

    def send_a(u):
        a_copy(u, 0).start()
        a_copy(u, 1).start()

    def raw(u):
        for side, step in ((0, 1), (1, 3)):
            value = term(u, (y + step) % 4)
            through, direct = (value[:128], value[128:]) if side == 0 else (value[128:], value[:128])
            sb[u, side, (hi, lo)[side], :] = direct.astype(BF16)
            b_copy(u, side, 1 - side).start()
            part[u % 2, side] = through

    def add(u):
        for side in (0, 1):
            a_copy(u, side).wait_recv()
            rows = (lo, hi)[side]
            sb[u, side, rows, :] = (part[u % 2, side] + ra[u, rows, :].astype(F32)).astype(BF16)
            b_copy(u, side, side).start()

    def finish(u):
        own = term(u, y)
        for side in (0, 1):
            for half in (0, 1):
                b_copy(u, side, half).wait_recv()
        total = own + rb[u, 0].astype(F32) + rb[u, 1].astype(F32)
        rows = pl.ds(u % 2 * 256, 256)
        if u in (0, 1, 4):
            sc[min(u, 2)] = total.astype(BF16)
            c_copy(u).start()
        elif u < 4:
            c_copy(u - 2).wait_recv()
            total = total + rc[u - 2].astype(F32)
            product = total[:, :128] * total[:, 128:]
            gat[rows, :] = product
            for half in (0, 1):
                s = u % 2 * 2 + half
                g32[pl.ds(s, 128, stride=4), :] = jnp.transpose(product[half * 128:half * 128 + 128, :])
        else:
            c_copy(4).wait_recv()
            total = total + rc[2].astype(F32)
            query[pl.ds(0, 256), :] = total[:, :128]
            query[pl.ds(256, 256), :] = total[:, 128:]

    def spread(src, dst, which, first=1, last=32):
        def go(k, carry):
            to = (me // 8 + k // 8) % 4 * 8 + (me + k) % 8
            remote(src.at[to], dst.at[me], x_send.at[which], x_recv.at[which], (to, t)).start()
            return carry

        lax.fori_loop(max(first, 8), last, go, 0)
        if first == 1:
            lax.fori_loop(1, 8, go, 0)
            dst[me] = src[me]

    def arrived(dst, which):
        others = dst.at[pl.ds(0, 31)]
        pltpu.make_async_copy(others, others, x_recv.at[which]).wait()

    def left(src, which):
        others = src.at[pl.ds(0, 31)]
        pltpu.make_async_copy(others, others, x_send.at[which]).wait()

    def ahead(u):
        compute_a(u)
        send_a(u)

    def arrange_response():
        need(1)
        for ri in range(2):
            for b in range(8):
                hs32[pl.ds(ri * 8 + b, 128, stride=16), :] = jnp.transpose(rsp[ri, pl.ds(b, 128, stride=8), :])
        hs[...] = hs32[...].astype(BF16).reshape(32, 64, 128)

    def send_gated():
        gs[...] = g32[...].astype(BF16).reshape(32, 16, 128)
        spread(gs, gr, 1)

    arrange_response()
    need(4)
    compute_a(0)
    pl.semaphore_wait(barrier, 34)
    send_a(0)
    raw(0)
    spread(hs, hr, 0)
    ahead(1)
    add(0)
    raw(1)
    ahead(2)
    add(1)
    raw(2)
    finish(0)
    ahead(3)
    add(2)
    raw(3)
    finish(1)
    need(10)
    ahead(4)
    add(3)
    raw(4)
    ahead(5)
    finish(2)
    add(4)
    raw(5)
    finish(3)
    send_gated()
    add(5)
    finish(4)
    arrived(hr, 0)
    arrived(gr, 1)

    g32[...] = gr[...].astype(F32).reshape(512, 128)
    signal = jnp.concatenate(
        [jnp.concatenate([g32[pl.ds(c * 4 + s, 32, stride=16), :] for s in range(4)], axis=0) for c in range(4)],
        axis=1).astype(BF16)
    mid = jnp.dot(f1[...], signal, preferred_element_type=F32)
    cosine, sine = tw[0], tw[1]
    waves = []
    for c in range(4):
        lanes = slice(c * 128, c * 128 + 128)
        re, im = mid[:256, lanes], mid[256:, lanes]
        turned = jnp.concatenate([re * cosine + im * sine, im * cosine - re * sine], axis=1).astype(BF16)
        spec = jnp.dot(turned, f2[...], preferred_element_type=F32)
        resp = hr[:, 16 * c:16 * c + 16, :].astype(F32)
        resp_re = resp[:, :8, :].reshape(256, 128)
        resp_im = resp[:, 8:, :].reshape(256, 128)
        re, im = spec[:, :128], spec[:, 128:]
        filtered = jnp.concatenate([re * resp_re - im * resp_im, re * resp_im + im * resp_re], axis=1).astype(BF16)
        back = jnp.dot(filtered, g2[...], preferred_element_type=F32)
        re, im = back[:, :128], back[:, 128:]
        waves.append(jnp.concatenate([re * cosine - im * sine, re * sine + im * cosine], axis=0).astype(BF16))
    conv = jnp.dot(g1[...], jnp.concatenate(waves, axis=1), preferred_element_type=F32)
    for c in range(4):
        for s in range(4):
            g32[pl.ds(c * 4 + s, 32, stride=16), :] = conv[s * 32:s * 32 + 32, c * 128:c * 128 + 128]
    cs[...] = g32[...].astype(BF16).reshape(32, 16, 128)
    spread(cs, cr, 2)

    finish(5)
    gain = skip_ref[...]
    arrived(cr, 2)
    g32[...] = cr[...].astype(F32).reshape(512, 128)
    for s in range(4):
        rows = pl.ds(s * 128, 128)
        conv_rows = jnp.transpose(g32[pl.ds(s, 128, stride=4), :])
        o_ref[rows, :] = (query[rows, :] * (conv_rows + gain * gat[rows, :])).astype(BF16)

    for u in range(UNITS):
        for side in (0, 1):
            a_copy(u, side).wait_send()
            for half in (0, 1):
                b_copy(u, side, half).wait_send()
    for u in (0, 1, 4):
        c_copy(u).wait_send()
    for src, which in ((hs, 0), (gs, 1), (cs, 2)):
        left(src, which)


def per_device(tokens, in_weight, skip_gain, response):
    first, second, back, last, twist = tables()
    anywhere = pl.BlockSpec(memory_space=pltpu.HBM)
    vmem = pl.BlockSpec(memory_space=pltpu.VMEM)
    return pl.pallas_call(
        kernel,
        out_shape=jax.ShapeDtypeStruct((512, 128), BF16),
        in_specs=[anywhere, anywhere, vmem] + [anywhere] * 6,
        out_specs=vmem,
        scratch_shapes=[
            pltpu.VMEM((512, 1024), BF16),
            pltpu.VMEM((3, 1024, 1024), BF16),
            pltpu.VMEM((2, 1024, 128), F32),
            pltpu.VMEM((512, 128), BF16),
            pltpu.VMEM((256, 256), BF16),
            pltpu.VMEM((256, 256), BF16),
            pltpu.VMEM((128, 512), BF16),
            pltpu.VMEM((2, 256, 128), F32),
            pltpu.VMEM((UNITS, 256, 256), BF16),
            pltpu.VMEM((UNITS, 256, 256), BF16),
            pltpu.VMEM((UNITS, 2, 256, 256), BF16),
            pltpu.VMEM((UNITS, 2, 256, 256), BF16),
            pltpu.VMEM((3, 256, 256), BF16),
            pltpu.VMEM((3, 256, 256), BF16),
            pltpu.VMEM((2, 2, 128, 256), F32),
            pltpu.VMEM((512, 128), F32),
            pltpu.VMEM((512, 128), F32),
            pltpu.VMEM((2048, 128), F32),
            pltpu.VMEM((32, 64, 128), BF16),
            pltpu.VMEM((32, 64, 128), BF16),
            pltpu.VMEM((512, 128), F32),
            pltpu.VMEM((32, 16, 128), BF16),
            pltpu.VMEM((32, 16, 128), BF16),
            pltpu.VMEM((32, 16, 128), BF16),
            pltpu.VMEM((32, 16, 128), BF16),
            pltpu.SemaphoreType.DMA((10,)),
            pltpu.SemaphoreType.DMA((UNITS, 2)),
            pltpu.SemaphoreType.DMA((UNITS, 2)),
            pltpu.SemaphoreType.DMA((UNITS, 4)),
            pltpu.SemaphoreType.DMA((UNITS, 4)),
            pltpu.SemaphoreType.DMA((3,)),
            pltpu.SemaphoreType.DMA((3,)),
            pltpu.SemaphoreType.DMA((3,)),
            pltpu.SemaphoreType.DMA((3,)),
        ],
        compiler_params=pltpu.CompilerParams(
            collective_id=0, has_side_effects=True, vmem_limit_bytes=60 * 1024 * 1024
        ),
        cost_estimate=pl.CostEstimate(flops=4_000_000_000, bytes_accessed=9_000_000, transcendentals=0),
    )(tokens, jnp.transpose(in_weight, (1, 0, 2)), skip_gain.reshape(1, 128), response.reshape(2, 1024, 128),
      first, second, back, last, twist)


def solution(mesh):
    in_specs = (P("ctx", "tp"), P("tp", None, None), P("tp"), P(None, None, "ctx", "tp"))
    return jax.shard_map(
        per_device, mesh=mesh, in_specs=in_specs, out_specs=P("ctx", "tp"), check_vma=False
    )
```

```python
import functools
import math

import jax
import jax.numpy as jnp
import numpy as np
from jax import lax
from jax.experimental import pallas as pl
from jax.experimental.pallas import tpu as pltpu
from jax.sharding import PartitionSpec as P

MESH = pl.DeviceIdType.MESH
F32 = jnp.float32
BF16 = jnp.bfloat16
UNITS = 6


def tables():
    row = np.arange(256)
    dev, inner = row // 8, row % 8
    rev = sum(((dev >> level) & 1) << (4 - level) for level in range(5))
    k1 = 2 * rev + inner % 2 + 64 * (inner // 2)
    col = np.arange(128)
    n1 = 4 * (col % 32) + col // 32
    n2 = np.arange(128)
    ang1 = 2 * np.pi / 256 * (k1[:, None] * n1[None, :] % 256)
    first = np.concatenate([np.cos(ang1), -np.sin(ang1)], axis=0)
    last = np.concatenate([np.cos(ang1).T, -np.sin(ang1).T], axis=1) / 32768
    ang2 = 2 * np.pi / 128 * (n2[:, None] * n2[None, :] % 128)
    c2, s2 = np.cos(ang2), np.sin(ang2)
    second = np.block([[c2, -s2], [s2, c2]])
    back = np.block([[c2, s2], [-s2, c2]])
    tw = 2 * np.pi / 32768 * (k1[:, None] * n2[None, :])
    bf = lambda a: jnp.asarray(a.astype(np.float32).astype(BF16))
    twist = jnp.asarray(np.stack([np.cos(tw), np.sin(tw)]).astype(np.float32))
    return bf(first), bf(second), bf(back), bf(last), twist


def kernel(tok_h, w_h, skip_ref, rsp_h, f1_h, f2_h, g2_h, g1_h, tw_h, o_ref,
           tok, w, rsp, f1, f2, g2, g1, tw,
           sa, ra, sb, rb, sc, rc, part, gat, query,
           hs32, hs, hr, g32, gs, gr, cs, cr,
           load_sem, sa_sem, ra_sem, sb_sem, rb_sem, sc_sem, rc_sem, x_send, x_recv):
    me = lax.axis_index("ctx")
    t = lax.axis_index("tp")
    zh, y = t // 4, t % 4
    up = (me, zh * 4 + (y + 1) % 4)
    down = (me, zh * 4 + (y + 3) % 4)
    across = (me, (1 - zh) * 4 + y)

    def columns(z, dest_y):
        return pl.ds(pl.multiple_of((z * 4 + dest_y) * 128, 128), 128)

    far, near = 1 - zh, zh
    pieces = [(rsp_h, rsp), (tok_h, tok), (w_h.at[1], w.at[1]), (w_h.at[2], w.at[2]), (w_h.at[0], w.at[0]),
              (f1_h, f1), (f2_h, f2), (g2_h, g2), (g1_h, g1), (tw_h, tw)]
    loads = [pltpu.make_async_copy(src, dst, load_sem.at[i]) for i, (src, dst) in enumerate(pieces)]
    for copy in loads:
        copy.start()
    waited = []

    def need(count):
        while len(waited) < count:
            loads[len(waited)].wait()
            waited.append(True)

    barrier = pltpu.get_barrier_semaphore()
    for dev in (up, down, across):
        pl.semaphore_signal(barrier, inc=1, device_id=dev, device_id_type=MESH)

    def greet(k, carry):
        pl.semaphore_signal(barrier, inc=1, device_id=((me + k) % 32, t), device_id_type=MESH)
        return carry

    lax.fori_loop(1, 32, greet, 0)

    def term(u, dest_y):
        if u >= 4:
            value = jnp.dot(tok[...], w[0, :, columns((far, near)[u - 4], dest_y)], preferred_element_type=F32)
            return jnp.concatenate([value[:256], value[256:]], axis=1)
        rows = pl.ds(u % 2 * 256, 256)
        if u < 2:
            rhs = [w[1, :, columns(far, dest_y)], w[2, :, columns(far, dest_y)]]
        else:
            rhs = [w[1, :, columns(near, dest_y)], w[2, :, columns(near, dest_y)]]
        return jnp.dot(tok[rows, :], jnp.concatenate(rhs, axis=1), preferred_element_type=F32)

    def remote(src, dst, ssem, rsem, dev):
        return pltpu.make_async_remote_copy(src_ref=src, dst_ref=dst, send_sem=ssem, recv_sem=rsem,
                                            device_id=dev, device_id_type=MESH)

    lo, hi = pl.ds(0, 128), pl.ds(128, 128)

    def a_copy(u, side):
        part_rows = (lo, hi)[side]
        return remote(sa.at[u, part_rows], ra.at[u, part_rows], sa_sem.at[u, side], ra_sem.at[u, side], (up, down)[side])

    def b_copy(u, side, half):
        part_rows = (lo, hi)[half]
        return remote(sb.at[u, side, part_rows], rb.at[u, side, part_rows], sb_sem.at[u, 2 * side + half],
                      rb_sem.at[u, 2 * side + half], (up, down)[side])

    def c_copy(u):
        slot = min(u, 2)
        return remote(sc.at[slot], rc.at[slot], sc_sem.at[slot], rc_sem.at[slot], across)

    def compute_a(u):
        sa[u] = term(u, (y + 2) % 4).astype(BF16)

    def send_a(u):
        a_copy(u, 0).start()
        a_copy(u, 1).start()

    def raw(u):
        for side, step in ((0, 1), (1, 3)):
            value = term(u, (y + step) % 4)
            through, direct = (value[:128], value[128:]) if side == 0 else (value[128:], value[:128])
            sb[u, side, (hi, lo)[side], :] = direct.astype(BF16)
            b_copy(u, side, 1 - side).start()
            part[u % 2, side] = through

    def add(u):
        for side in (0, 1):
            a_copy(u, side).wait_recv()
            rows = (lo, hi)[side]
            sb[u, side, rows, :] = (part[u % 2, side] + ra[u, rows, :].astype(F32)).astype(BF16)
            b_copy(u, side, side).start()

    def finish(u):
        own = term(u, y)
        for side in (0, 1):
            for half in (0, 1):
                b_copy(u, side, half).wait_recv()
        total = own + rb[u, 0].astype(F32) + rb[u, 1].astype(F32)
        rows = pl.ds(u % 2 * 256, 256)
        if u in (0, 1, 4):
            sc[min(u, 2)] = total.astype(BF16)
            c_copy(u).start()
        elif u < 4:
            c_copy(u - 2).wait_recv()
            total = total + rc[u - 2].astype(F32)
            product = total[:, :128] * total[:, 128:]
            gat[rows, :] = product
            for half in (0, 1):
                s = u % 2 * 2 + half
                g32[pl.ds(s, 128, stride=4), :] = jnp.transpose(product[half * 128:half * 128 + 128, :])
        else:
            c_copy(4).wait_recv()
            total = total + rc[2].astype(F32)
            query[pl.ds(0, 256), :] = total[:, :128]
            query[pl.ds(256, 256), :] = total[:, 128:]

    def spread(src, dst, which, first=1, last=32):
        def go(k, carry):
            to = (me // 8 + k // 8) % 4 * 8 + (me + k) % 8
            remote(src.at[to], dst.at[me], x_send.at[which], x_recv.at[which], (to, t)).start()
            return carry

        lax.fori_loop(max(first, 8), last, go, 0)
        if first == 1:
            lax.fori_loop(1, 8, go, 0)
            dst[me] = src[me]

    def arrived(dst, which):
        others = dst.at[pl.ds(0, 31)]
        pltpu.make_async_copy(others, others, x_recv.at[which]).wait()

    def left(src, which):
        others = src.at[pl.ds(0, 31)]
        pltpu.make_async_copy(others, others, x_send.at[which]).wait()

    def ahead(u):
        compute_a(u)
        send_a(u)

    def arrange_response():
        need(1)
        for ri in range(2):
            for b in range(8):
                hs32[pl.ds(ri * 8 + b, 128, stride=16), :] = jnp.transpose(rsp[ri, pl.ds(b, 128, stride=8), :])
        hs[...] = hs32[...].astype(BF16).reshape(32, 64, 128)

    def send_gated():
        gs[...] = g32[...].astype(BF16).reshape(32, 16, 128)
        spread(gs, gr, 1)

    arrange_response()
    need(4)
    compute_a(0)
    pl.semaphore_wait(barrier, 34)
    send_a(0)
    spread(hs, hr, 0)
    raw(0)
    ahead(1)
    add(0)
    raw(1)
    add(1)
    ahead(2)
    finish(0)
    raw(2)
    finish(1)
    add(2)
    ahead(3)
    raw(3)
    add(3)
    need(10)
    ahead(4)
    raw(4)
    finish(2)
    ahead(5)
    add(4)
    raw(5)
    finish(3)
    send_gated()
    add(5)
    finish(4)
    arrived(hr, 0)
    arrived(gr, 1)

    g32[...] = gr[...].astype(F32).reshape(512, 128)
    signal = jnp.concatenate(
        [jnp.concatenate([g32[pl.ds(c * 4 + s, 32, stride=16), :] for s in range(4)], axis=0) for c in range(4)],
        axis=1).astype(BF16)
    mid = jnp.dot(f1[...], signal, preferred_element_type=F32)
    cosine, sine = tw[0], tw[1]
    waves = []
    for c in range(4):
        lanes = slice(c * 128, c * 128 + 128)
        re, im = mid[:256, lanes], mid[256:, lanes]
        turned = jnp.concatenate([re * cosine + im * sine, im * cosine - re * sine], axis=1).astype(BF16)
        spec = jnp.dot(turned, f2[...], preferred_element_type=F32)
        resp = hr[:, 16 * c:16 * c + 16, :].astype(F32)
        resp_re = resp[:, :8, :].reshape(256, 128)
        resp_im = resp[:, 8:, :].reshape(256, 128)
        re, im = spec[:, :128], spec[:, 128:]
        filtered = jnp.concatenate([re * resp_re - im * resp_im, re * resp_im + im * resp_re], axis=1).astype(BF16)
        back = jnp.dot(filtered, g2[...], preferred_element_type=F32)
        re, im = back[:, :128], back[:, 128:]
        waves.append(jnp.concatenate([re * cosine - im * sine, re * sine + im * cosine], axis=0).astype(BF16))
    conv = jnp.dot(g1[...], jnp.concatenate(waves, axis=1), preferred_element_type=F32)
    for c in range(4):
        for s in range(4):
            g32[pl.ds(c * 4 + s, 32, stride=16), :] = conv[s * 32:s * 32 + 32, c * 128:c * 128 + 128]
    cs[...] = g32[...].astype(BF16).reshape(32, 16, 128)
    spread(cs, cr, 2)

    finish(5)
    gain = skip_ref[...]
    arrived(cr, 2)
    g32[...] = cr[...].astype(F32).reshape(512, 128)
    for s in range(4):
        rows = pl.ds(s * 128, 128)
        conv_rows = jnp.transpose(g32[pl.ds(s, 128, stride=4), :])
        o_ref[rows, :] = (query[rows, :] * (conv_rows + gain * gat[rows, :])).astype(BF16)

    for u in range(UNITS):
        for side in (0, 1):
            a_copy(u, side).wait_send()
            for half in (0, 1):
                b_copy(u, side, half).wait_send()
    for u in (0, 1, 4):
        c_copy(u).wait_send()
    for src, which in ((hs, 0), (gs, 1), (cs, 2)):
        left(src, which)


def per_device(tokens, in_weight, skip_gain, response):
    first, second, back, last, twist = tables()
    anywhere = pl.BlockSpec(memory_space=pltpu.HBM)
    vmem = pl.BlockSpec(memory_space=pltpu.VMEM)
    return pl.pallas_call(
        kernel,
        out_shape=jax.ShapeDtypeStruct((512, 128), BF16),
        in_specs=[anywhere, anywhere, vmem] + [anywhere] * 6,
        out_specs=vmem,
        scratch_shapes=[
            pltpu.VMEM((512, 1024), BF16),
            pltpu.VMEM((3, 1024, 1024), BF16),
            pltpu.VMEM((2, 1024, 128), F32),
            pltpu.VMEM((512, 128), BF16),
            pltpu.VMEM((256, 256), BF16),
            pltpu.VMEM((256, 256), BF16),
            pltpu.VMEM((128, 512), BF16),
            pltpu.VMEM((2, 256, 128), F32),
            pltpu.VMEM((UNITS, 256, 256), BF16),
            pltpu.VMEM((UNITS, 256, 256), BF16),
            pltpu.VMEM((UNITS, 2, 256, 256), BF16),
            pltpu.VMEM((UNITS, 2, 256, 256), BF16),
            pltpu.VMEM((3, 256, 256), BF16),
            pltpu.VMEM((3, 256, 256), BF16),
            pltpu.VMEM((2, 2, 128, 256), F32),
            pltpu.VMEM((512, 128), F32),
            pltpu.VMEM((512, 128), F32),
            pltpu.VMEM((2048, 128), F32),
            pltpu.VMEM((32, 64, 128), BF16),
            pltpu.VMEM((32, 64, 128), BF16),
            pltpu.VMEM((512, 128), F32),
            pltpu.VMEM((32, 16, 128), BF16),
            pltpu.VMEM((32, 16, 128), BF16),
            pltpu.VMEM((32, 16, 128), BF16),
            pltpu.VMEM((32, 16, 128), BF16),
            pltpu.SemaphoreType.DMA((10,)),
            pltpu.SemaphoreType.DMA((UNITS, 2)),
            pltpu.SemaphoreType.DMA((UNITS, 2)),
            pltpu.SemaphoreType.DMA((UNITS, 4)),
            pltpu.SemaphoreType.DMA((UNITS, 4)),
            pltpu.SemaphoreType.DMA((3,)),
            pltpu.SemaphoreType.DMA((3,)),
            pltpu.SemaphoreType.DMA((3,)),
            pltpu.SemaphoreType.DMA((3,)),
        ],
        compiler_params=pltpu.CompilerParams(
            collective_id=0, has_side_effects=True, vmem_limit_bytes=60 * 1024 * 1024
        ),
        cost_estimate=pl.CostEstimate(flops=4_000_000_000, bytes_accessed=9_000_000, transcendentals=0),
    )(tokens, jnp.transpose(in_weight, (1, 0, 2)), skip_gain.reshape(1, 128), response.reshape(2, 1024, 128),
      first, second, back, last, twist)


def solution(mesh):
    in_specs = (P("ctx", "tp"), P("tp", None, None), P("tp"), P(None, None, "ctx", "tp"))
    return jax.shard_map(
        per_device, mesh=mesh, in_specs=in_specs, out_specs=P("ctx", "tp"), check_vma=False
    )
```

```python
import functools
import math

import jax
import jax.numpy as jnp
import numpy as np
from jax import lax
from jax.experimental import pallas as pl
from jax.experimental.pallas import tpu as pltpu
from jax.sharding import PartitionSpec as P

MESH = pl.DeviceIdType.MESH
F32 = jnp.float32
BF16 = jnp.bfloat16
UNITS = 6


def tables():
    row = np.arange(256)
    dev, inner = row // 8, row % 8
    rev = sum(((dev >> level) & 1) << (4 - level) for level in range(5))
    k1 = 2 * rev + inner % 2 + 64 * (inner // 2)
    col = np.arange(128)
    n1 = 4 * (col % 32) + col // 32
    n2 = np.arange(128)
    ang1 = 2 * np.pi / 256 * (k1[:, None] * n1[None, :] % 256)
    first = np.concatenate([np.cos(ang1), -np.sin(ang1)], axis=0)
    last = np.concatenate([np.cos(ang1).T, -np.sin(ang1).T], axis=1) / 32768
    ang2 = 2 * np.pi / 128 * (n2[:, None] * n2[None, :] % 128)
    c2, s2 = np.cos(ang2), np.sin(ang2)
    second = np.block([[c2, -s2], [s2, c2]])
    back = np.block([[c2, s2], [-s2, c2]])
    tw = 2 * np.pi / 32768 * (k1[:, None] * n2[None, :])
    bf = lambda a: jnp.asarray(a.astype(np.float32).astype(BF16))
    twist = jnp.asarray(np.stack([np.cos(tw), np.sin(tw)]).astype(np.float32))
    return bf(first), bf(second), bf(back), bf(last), twist


def kernel(tok_h, w_h, skip_ref, rsp_h, f1_h, f2_h, g2_h, g1_h, tw_h, o_ref,
           tok, w, rsp, f1, f2, g2, g1, tw,
           sa, ra, sb, rb, sc, rc, part, gat, query,
           hs32, hs, hr, g32, gs, gr, cs, cr,
           load_sem, sa_sem, ra_sem, sb_sem, rb_sem, sc_sem, rc_sem, x_send, x_recv, z_ready):
    me = lax.axis_index("ctx")
    t = lax.axis_index("tp")
    zh, y = t // 4, t % 4
    up = (me, zh * 4 + (y + 1) % 4)
    down = (me, zh * 4 + (y + 3) % 4)
    across = (me, (1 - zh) * 4 + y)

    def columns(z, dest_y):
        return pl.ds(pl.multiple_of((z * 4 + dest_y) * 128, 128), 128)

    far, near = 1 - zh, zh
    pieces = [(rsp_h, rsp), (tok_h, tok), (w_h.at[1], w.at[1]), (w_h.at[2], w.at[2]), (w_h.at[0], w.at[0]),
              (f1_h, f1), (f2_h, f2), (g2_h, g2), (g1_h, g1), (tw_h, tw)]
    loads = [pltpu.make_async_copy(src, dst, load_sem.at[i]) for i, (src, dst) in enumerate(pieces)]
    for copy in loads:
        copy.start()
    waited = []

    def need(count):
        while len(waited) < count:
            loads[len(waited)].wait()
            waited.append(True)

    barrier = pltpu.get_barrier_semaphore()
    for dev in (up, down):
        pl.semaphore_signal(barrier, inc=1, device_id=dev, device_id_type=MESH)

    @pl.when(zh == 0)
    def _():
        pl.semaphore_signal(barrier, inc=1, device_id=across, device_id_type=MESH)

    def greet(k, carry):
        pl.semaphore_signal(barrier, inc=1, device_id=((me + k) % 32, t), device_id_type=MESH)
        return carry

    lax.fori_loop(1, 32, greet, 0)

    def enter():
        pl.semaphore_wait(barrier, 33 + zh)

        @pl.when(zh == 1)
        def _():
            pl.semaphore_signal(z_ready, inc=1, device_id=across, device_id_type=MESH)

    def across_present():
        @pl.when(zh == 0)
        def _():
            pl.semaphore_wait(z_ready, 1)

    def term(u, dest_y):
        if u >= 4:
            value = jnp.dot(tok[...], w[0, :, columns((far, near)[u - 4], dest_y)], preferred_element_type=F32)
            return jnp.concatenate([value[:256], value[256:]], axis=1)
        rows = pl.ds(u % 2 * 256, 256)
        if u < 2:
            rhs = [w[1, :, columns(far, dest_y)], w[2, :, columns(far, dest_y)]]
        else:
            rhs = [w[1, :, columns(near, dest_y)], w[2, :, columns(near, dest_y)]]
        return jnp.dot(tok[rows, :], jnp.concatenate(rhs, axis=1), preferred_element_type=F32)

    def remote(src, dst, ssem, rsem, dev):
        return pltpu.make_async_remote_copy(src_ref=src, dst_ref=dst, send_sem=ssem, recv_sem=rsem,
                                            device_id=dev, device_id_type=MESH)

    lo, hi = pl.ds(0, 128), pl.ds(128, 128)

    def a_copy(u, side):
        part_rows = (lo, hi)[side]
        return remote(sa.at[u, part_rows], ra.at[u, part_rows], sa_sem.at[u, side], ra_sem.at[u, side], (up, down)[side])

    def b_copy(u, side, half):
        part_rows = (lo, hi)[half]
        return remote(sb.at[u, side, part_rows], rb.at[u, side, part_rows], sb_sem.at[u, 2 * side + half],
                      rb_sem.at[u, 2 * side + half], (up, down)[side])

    def c_copy(u):
        slot = min(u, 2)
        return remote(sc.at[slot], rc.at[slot], sc_sem.at[slot], rc_sem.at[slot], across)

    def compute_a(u):
        sa[u] = term(u, (y + 2) % 4).astype(BF16)

    def send_a(u):
        a_copy(u, 0).start()
        a_copy(u, 1).start()

    def raw(u):
        for side, step in ((0, 1), (1, 3)):
            value = term(u, (y + step) % 4)
            through, direct = (value[:128], value[128:]) if side == 0 else (value[128:], value[:128])
            sb[u, side, (hi, lo)[side], :] = direct.astype(BF16)
            b_copy(u, side, 1 - side).start()
            part[u % 2, side] = through

    def add(u):
        for side in (0, 1):
            a_copy(u, side).wait_recv()
            rows = (lo, hi)[side]
            sb[u, side, rows, :] = (part[u % 2, side] + ra[u, rows, :].astype(F32)).astype(BF16)
            b_copy(u, side, side).start()

    def finish(u):
        own = term(u, y)
        for side in (0, 1):
            for half in (0, 1):
                b_copy(u, side, half).wait_recv()
        total = own + rb[u, 0].astype(F32) + rb[u, 1].astype(F32)
        rows = pl.ds(u % 2 * 256, 256)
        if u in (0, 1, 4):
            sc[min(u, 2)] = total.astype(BF16)
            c_copy(u).start()
        elif u < 4:
            c_copy(u - 2).wait_recv()
            total = total + rc[u - 2].astype(F32)
            product = total[:, :128] * total[:, 128:]
            gat[rows, :] = product
            for half in (0, 1):
                s = u % 2 * 2 + half
                g32[pl.ds(s, 128, stride=4), :] = jnp.transpose(product[half * 128:half * 128 + 128, :])
        else:
            c_copy(4).wait_recv()
            total = total + rc[2].astype(F32)
            query[pl.ds(0, 256), :] = total[:, :128]
            query[pl.ds(256, 256), :] = total[:, 128:]

    def spread(src, dst, which):
        def go(k, carry):
            to = (me // 8 + k // 8) % 4 * 8 + (me + k) % 8
            remote(src.at[to], dst.at[me], x_send.at[which], x_recv.at[which], (to, t)).start()
            return carry

        lax.fori_loop(8, 32, go, 0)
        lax.fori_loop(1, 8, go, 0)
        dst[me] = src[me]

    def arrived(dst, which):
        others = dst.at[pl.ds(0, 31)]
        pltpu.make_async_copy(others, others, x_recv.at[which]).wait()

    def left(src, which):
        others = src.at[pl.ds(0, 31)]
        pltpu.make_async_copy(others, others, x_send.at[which]).wait()

    def ahead(u):
        compute_a(u)
        send_a(u)

    def arrange_response():
        need(1)
        for ri in range(2):
            for b in range(8):
                hs32[pl.ds(ri * 8 + b, 128, stride=16), :] = jnp.transpose(rsp[ri, pl.ds(b, 128, stride=8), :])
        hs[...] = hs32[...].astype(BF16).reshape(32, 64, 128)

    def send_gated():
        gs[...] = g32[...].astype(BF16).reshape(32, 16, 128)
        spread(gs, gr, 1)

    arrange_response()
    need(4)
    compute_a(0)
    enter()
    send_a(0)
    spread(hs, hr, 0)
    raw(0)
    ahead(1)
    add(0)
    raw(1)
    add(1)
    ahead(2)
    across_present()
    finish(0)
    raw(2)
    finish(1)
    add(2)
    ahead(3)
    raw(3)
    add(3)
    need(10)
    ahead(4)
    raw(4)
    finish(2)
    ahead(5)
    add(4)
    raw(5)
    finish(3)
    send_gated()
    add(5)
    finish(4)
    arrived(hr, 0)
    arrived(gr, 1)

    g32[...] = gr[...].astype(F32).reshape(512, 128)
    signal = jnp.concatenate(
        [jnp.concatenate([g32[pl.ds(c * 4 + s, 32, stride=16), :] for s in range(4)], axis=0) for c in range(4)],
        axis=1).astype(BF16)
    mid = jnp.dot(f1[...], signal, preferred_element_type=F32)
    cosine, sine = tw[0], tw[1]
    waves = []
    for c in range(4):
        lanes = slice(c * 128, c * 128 + 128)
        re, im = mid[:256, lanes], mid[256:, lanes]
        turned = jnp.concatenate([re * cosine + im * sine, im * cosine - re * sine], axis=1).astype(BF16)
        spec = jnp.dot(turned, f2[...], preferred_element_type=F32)
        resp = hr[:, 16 * c:16 * c + 16, :].astype(F32)
        resp_re = resp[:, :8, :].reshape(256, 128)
        resp_im = resp[:, 8:, :].reshape(256, 128)
        re, im = spec[:, :128], spec[:, 128:]
        filtered = jnp.concatenate([re * resp_re - im * resp_im, re * resp_im + im * resp_re], axis=1).astype(BF16)
        back = jnp.dot(filtered, g2[...], preferred_element_type=F32)
        re, im = back[:, :128], back[:, 128:]
        waves.append(jnp.concatenate([re * cosine - im * sine, re * sine + im * cosine], axis=0).astype(BF16))
    conv = jnp.dot(g1[...], jnp.concatenate(waves, axis=1), preferred_element_type=F32)
    for c in range(4):
        for s in range(4):
            g32[pl.ds(c * 4 + s, 32, stride=16), :] = conv[s * 32:s * 32 + 32, c * 128:c * 128 + 128]
    cs[...] = g32[...].astype(BF16).reshape(32, 16, 128)
    spread(cs, cr, 2)

    finish(5)
    gain = skip_ref[...]
    arrived(cr, 2)
    g32[...] = cr[...].astype(F32).reshape(512, 128)
    for s in range(4):
        rows = pl.ds(s * 128, 128)
        conv_rows = jnp.transpose(g32[pl.ds(s, 128, stride=4), :])
        o_ref[rows, :] = (query[rows, :] * (conv_rows + gain * gat[rows, :])).astype(BF16)

    for u in range(UNITS):
        for side in (0, 1):
            a_copy(u, side).wait_send()
            for half in (0, 1):
                b_copy(u, side, half).wait_send()
    for u in (0, 1, 4):
        c_copy(u).wait_send()
    for src, which in ((hs, 0), (gs, 1), (cs, 2)):
        left(src, which)


def per_device(tokens, in_weight, skip_gain, response):
    first, second, back, last, twist = tables()
    anywhere = pl.BlockSpec(memory_space=pltpu.HBM)
    vmem = pl.BlockSpec(memory_space=pltpu.VMEM)
    return pl.pallas_call(
        kernel,
        out_shape=jax.ShapeDtypeStruct((512, 128), BF16),
        in_specs=[anywhere, anywhere, vmem] + [anywhere] * 6,
        out_specs=vmem,
        scratch_shapes=[
            pltpu.VMEM((512, 1024), BF16),
            pltpu.VMEM((3, 1024, 1024), BF16),
            pltpu.VMEM((2, 1024, 128), F32),
            pltpu.VMEM((512, 128), BF16),
            pltpu.VMEM((256, 256), BF16),
            pltpu.VMEM((256, 256), BF16),
            pltpu.VMEM((128, 512), BF16),
            pltpu.VMEM((2, 256, 128), F32),
            pltpu.VMEM((UNITS, 256, 256), BF16),
            pltpu.VMEM((UNITS, 256, 256), BF16),
            pltpu.VMEM((UNITS, 2, 256, 256), BF16),
            pltpu.VMEM((UNITS, 2, 256, 256), BF16),
            pltpu.VMEM((3, 256, 256), BF16),
            pltpu.VMEM((3, 256, 256), BF16),
            pltpu.VMEM((2, 2, 128, 256), F32),
            pltpu.VMEM((512, 128), F32),
            pltpu.VMEM((512, 128), F32),
            pltpu.VMEM((2048, 128), F32),
            pltpu.VMEM((32, 64, 128), BF16),
            pltpu.VMEM((32, 64, 128), BF16),
            pltpu.VMEM((512, 128), F32),
            pltpu.VMEM((32, 16, 128), BF16),
            pltpu.VMEM((32, 16, 128), BF16),
            pltpu.VMEM((32, 16, 128), BF16),
            pltpu.VMEM((32, 16, 128), BF16),
            pltpu.SemaphoreType.DMA((10,)),
            pltpu.SemaphoreType.DMA((UNITS, 2)),
            pltpu.SemaphoreType.DMA((UNITS, 2)),
            pltpu.SemaphoreType.DMA((UNITS, 4)),
            pltpu.SemaphoreType.DMA((UNITS, 4)),
            pltpu.SemaphoreType.DMA((3,)),
            pltpu.SemaphoreType.DMA((3,)),
            pltpu.SemaphoreType.DMA((3,)),
            pltpu.SemaphoreType.DMA((3,)),
            pltpu.SemaphoreType.REGULAR,
        ],
        compiler_params=pltpu.CompilerParams(
            collective_id=0, has_side_effects=True, vmem_limit_bytes=60 * 1024 * 1024
        ),
        cost_estimate=pl.CostEstimate(flops=4_000_000_000, bytes_accessed=9_000_000, transcendentals=0),
    )(tokens, jnp.transpose(in_weight, (1, 0, 2)), skip_gain.reshape(1, 128), response.reshape(2, 1024, 128),
      first, second, back, last, twist)


def solution(mesh):
    in_specs = (P("ctx", "tp"), P("tp", None, None), P("tp"), P(None, None, "ctx", "tp"))
    return jax.shard_map(
        per_device, mesh=mesh, in_specs=in_specs, out_specs=P("ctx", "tp"), check_vma=False
    )
```

```python
import functools
import math

import jax
import jax.numpy as jnp
import numpy as np
from jax import lax
from jax.experimental import pallas as pl
from jax.experimental.pallas import tpu as pltpu
from jax.sharding import PartitionSpec as P

MESH = pl.DeviceIdType.MESH
F32 = jnp.float32
BF16 = jnp.bfloat16
UNITS = 6


def tables():
    row = np.arange(256)
    dev, inner = row // 8, row % 8
    rev = sum(((dev >> level) & 1) << (4 - level) for level in range(5))
    k1 = 2 * rev + inner % 2 + 64 * (inner // 2)
    col = np.arange(128)
    n1 = 4 * (col % 32) + col // 32
    n2 = np.arange(128)
    ang1 = 2 * np.pi / 256 * (k1[:, None] * n1[None, :] % 256)
    first = np.concatenate([np.cos(ang1), -np.sin(ang1)], axis=0)
    last = np.concatenate([np.cos(ang1).T, -np.sin(ang1).T], axis=1) / 32768
    ang2 = 2 * np.pi / 128 * (n2[:, None] * n2[None, :] % 128)
    c2, s2 = np.cos(ang2), np.sin(ang2)
    second = np.block([[c2, -s2], [s2, c2]])
    back = np.block([[c2, s2], [-s2, c2]])
    tw = 2 * np.pi / 32768 * (k1[:, None] * n2[None, :])
    bf = lambda a: jnp.asarray(a.astype(np.float32).astype(BF16))
    twist = jnp.asarray(np.stack([np.cos(tw), np.sin(tw)]).astype(np.float32))
    return bf(first), bf(second), bf(back), bf(last), twist


def kernel(tok_h, w_h, skip_ref, rsp_h, f1_h, f2_h, g2_h, g1_h, tw_h, o_ref,
           tok, w, rsp, f1, f2, g2, g1, tw,
           sa, ra, sb, rb, sc, rc, part, gat, query,
           hs32, hs, hr, g32, gs, gr, cs, cr,
           load_sem, sa_sem, ra_sem, sb_sem, rb_sem, sc_sem, rc_sem, x_send, x_recv, z_ready):
    me = lax.axis_index("ctx")
    t = lax.axis_index("tp")
    zh, y = t // 4, t % 4
    up = (me, zh * 4 + (y + 1) % 4)
    down = (me, zh * 4 + (y + 3) % 4)
    across = (me, (1 - zh) * 4 + y)

    def columns(z, dest_y):
        return pl.ds(pl.multiple_of((z * 4 + dest_y) * 128, 128), 128)

    far, near = 1 - zh, zh
    pieces = [(rsp_h, rsp), (tok_h, tok), (w_h.at[1], w.at[1]), (w_h.at[2], w.at[2]), (w_h.at[0], w.at[0]),
              (f1_h, f1), (f2_h, f2), (g2_h, g2), (g1_h, g1), (tw_h, tw)]
    loads = [pltpu.make_async_copy(src, dst, load_sem.at[i]) for i, (src, dst) in enumerate(pieces)]
    for copy in loads:
        copy.start()
    waited = []

    def need(count):
        while len(waited) < count:
            loads[len(waited)].wait()
            waited.append(True)

    barrier = pltpu.get_barrier_semaphore()
    for dev in (up, down):
        pl.semaphore_signal(barrier, inc=1, device_id=dev, device_id_type=MESH)

    @pl.when(zh == 0)
    def _():
        pl.semaphore_signal(barrier, inc=1, device_id=across, device_id_type=MESH)

    def greet(k, carry):
        pl.semaphore_signal(barrier, inc=1, device_id=((me + k) % 32, t), device_id_type=MESH)
        return carry

    lax.fori_loop(1, 32, greet, 0)

    def enter():
        pl.semaphore_wait(barrier, 33 + zh)

        @pl.when(zh == 1)
        def _():
            pl.semaphore_signal(z_ready, inc=1, device_id=across, device_id_type=MESH)

    def across_present():
        @pl.when(zh == 0)
        def _():
            pl.semaphore_wait(z_ready, 1)

    def term(u, dest_y):
        if u >= 4:
            value = jnp.dot(tok[...], w[0, :, columns((far, near)[u - 4], dest_y)], preferred_element_type=F32)
            return jnp.concatenate([value[:256], value[256:]], axis=1)
        rows = pl.ds(u % 2 * 256, 256)
        if u < 2:
            rhs = [w[1, :, columns(far, dest_y)], w[2, :, columns(far, dest_y)]]
        else:
            rhs = [w[1, :, columns(near, dest_y)], w[2, :, columns(near, dest_y)]]
        return jnp.dot(tok[rows, :], jnp.concatenate(rhs, axis=1), preferred_element_type=F32)

    def remote(src, dst, ssem, rsem, dev):
        return pltpu.make_async_remote_copy(src_ref=src, dst_ref=dst, send_sem=ssem, recv_sem=rsem,
                                            device_id=dev, device_id_type=MESH)

    lo, hi = pl.ds(0, 128), pl.ds(128, 128)

    def a_copy(u, side):
        part_rows = (lo, hi)[side]
        return remote(sa.at[u, part_rows], ra.at[u, part_rows], sa_sem.at[u, side], ra_sem.at[u, side], (up, down)[side])

    def b_copy(u, side, half):
        part_rows = (lo, hi)[half]
        return remote(sb.at[u, side, part_rows], rb.at[u, side, part_rows], sb_sem.at[u, 2 * side + half],
                      rb_sem.at[u, 2 * side + half], (up, down)[side])

    def c_copy(u):
        slot = min(u, 2)
        return remote(sc.at[slot], rc.at[slot], sc_sem.at[slot], rc_sem.at[slot], across)

    def compute_a(u):
        sa[u] = term(u, (y + 2) % 4).astype(BF16)

    def send_a(u):
        a_copy(u, 0).start()
        a_copy(u, 1).start()

    def raw(u):
        for side, step in ((0, 1), (1, 3)):
            value = term(u, (y + step) % 4)
            through, direct = (value[:128], value[128:]) if side == 0 else (value[128:], value[:128])
            sb[u, side, (hi, lo)[side], :] = direct.astype(BF16)
            b_copy(u, side, 1 - side).start()
            part[u % 2, side] = through

    def add(u):
        for side in (0, 1):
            a_copy(u, side).wait_recv()
            rows = (lo, hi)[side]
            sb[u, side, rows, :] = (part[u % 2, side] + ra[u, rows, :].astype(F32)).astype(BF16)
            b_copy(u, side, side).start()

    def finish(u):
        own = term(u, y)
        for side in (0, 1):
            for half in (0, 1):
                b_copy(u, side, half).wait_recv()
        total = own + rb[u, 0].astype(F32) + rb[u, 1].astype(F32)
        rows = pl.ds(u % 2 * 256, 256)
        if u in (0, 1, 4):
            sc[min(u, 2)] = total.astype(BF16)
            c_copy(u).start()
        elif u < 4:
            c_copy(u - 2).wait_recv()
            total = total + rc[u - 2].astype(F32)
            product = total[:, :128] * total[:, 128:]
            gat[rows, :] = product
            for half in (0, 1):
                s = u % 2 * 2 + half
                g32[pl.ds(s, 128, stride=4), :] = jnp.transpose(product[half * 128:half * 128 + 128, :])
        else:
            c_copy(4).wait_recv()
            total = total + rc[2].astype(F32)
            query[pl.ds(0, 256), :] = total[:, :128]
            query[pl.ds(256, 256), :] = total[:, 128:]

    def spread(src, dst, which):
        def go(k, carry):
            to = (me // 8 + k // 8) % 4 * 8 + (me + k) % 8
            remote(src.at[to], dst.at[me], x_send.at[which], x_recv.at[which], (to, t)).start()
            return carry

        lax.fori_loop(16, 24, go, 0)
        lax.fori_loop(8, 16, go, 0)
        lax.fori_loop(24, 32, go, 0)
        lax.fori_loop(1, 8, go, 0)
        dst[me] = src[me]

    def arrived(dst, which):
        others = dst.at[pl.ds(0, 31)]
        pltpu.make_async_copy(others, others, x_recv.at[which]).wait()

    def left(src, which):
        others = src.at[pl.ds(0, 31)]
        pltpu.make_async_copy(others, others, x_send.at[which]).wait()

    def ahead(u):
        compute_a(u)
        send_a(u)

    def arrange_response():
        need(1)
        for ri in range(2):
            for b in range(8):
                hs32[pl.ds(ri * 8 + b, 128, stride=16), :] = jnp.transpose(rsp[ri, pl.ds(b, 128, stride=8), :])
        hs[...] = hs32[...].astype(BF16).reshape(32, 64, 128)

    def send_gated():
        gs[...] = g32[...].astype(BF16).reshape(32, 16, 128)
        spread(gs, gr, 1)

    arrange_response()
    need(4)
    compute_a(0)
    enter()
    send_a(0)
    spread(hs, hr, 0)
    raw(0)
    ahead(1)
    add(0)
    raw(1)
    add(1)
    ahead(2)
    across_present()
    finish(0)
    raw(2)
    finish(1)
    add(2)
    ahead(3)
    raw(3)
    add(3)
    need(10)
    ahead(4)
    raw(4)
    finish(2)
    ahead(5)
    add(4)
    raw(5)
    finish(3)
    send_gated()
    add(5)
    finish(4)
    arrived(hr, 0)
    arrived(gr, 1)

    g32[...] = gr[...].astype(F32).reshape(512, 128)
    signal = jnp.concatenate(
        [jnp.concatenate([g32[pl.ds(c * 4 + s, 32, stride=16), :] for s in range(4)], axis=0) for c in range(4)],
        axis=1).astype(BF16)
    mid = jnp.dot(f1[...], signal, preferred_element_type=F32)
    cosine, sine = tw[0], tw[1]
    waves = []
    for c in range(4):
        lanes = slice(c * 128, c * 128 + 128)
        re, im = mid[:256, lanes], mid[256:, lanes]
        turned = jnp.concatenate([re * cosine + im * sine, im * cosine - re * sine], axis=1).astype(BF16)
        spec = jnp.dot(turned, f2[...], preferred_element_type=F32)
        resp = hr[:, 16 * c:16 * c + 16, :].astype(F32)
        resp_re = resp[:, :8, :].reshape(256, 128)
        resp_im = resp[:, 8:, :].reshape(256, 128)
        re, im = spec[:, :128], spec[:, 128:]
        filtered = jnp.concatenate([re * resp_re - im * resp_im, re * resp_im + im * resp_re], axis=1).astype(BF16)
        back = jnp.dot(filtered, g2[...], preferred_element_type=F32)
        re, im = back[:, :128], back[:, 128:]
        waves.append(jnp.concatenate([re * cosine - im * sine, re * sine + im * cosine], axis=0).astype(BF16))
    conv = jnp.dot(g1[...], jnp.concatenate(waves, axis=1), preferred_element_type=F32)
    for c in range(4):
        for s in range(4):
            g32[pl.ds(c * 4 + s, 32, stride=16), :] = conv[s * 32:s * 32 + 32, c * 128:c * 128 + 128]
    cs[...] = g32[...].astype(BF16).reshape(32, 16, 128)
    spread(cs, cr, 2)

    finish(5)
    gain = skip_ref[...]
    arrived(cr, 2)
    g32[...] = cr[...].astype(F32).reshape(512, 128)
    for s in range(4):
        rows = pl.ds(s * 128, 128)
        conv_rows = jnp.transpose(g32[pl.ds(s, 128, stride=4), :])
        o_ref[rows, :] = (query[rows, :] * (conv_rows + gain * gat[rows, :])).astype(BF16)

    for u in range(UNITS):
        for side in (0, 1):
            a_copy(u, side).wait_send()
            for half in (0, 1):
                b_copy(u, side, half).wait_send()
    for u in (0, 1, 4):
        c_copy(u).wait_send()
    for src, which in ((hs, 0), (gs, 1), (cs, 2)):
        left(src, which)


def per_device(tokens, in_weight, skip_gain, response):
    first, second, back, last, twist = tables()
    anywhere = pl.BlockSpec(memory_space=pltpu.HBM)
    vmem = pl.BlockSpec(memory_space=pltpu.VMEM)
    return pl.pallas_call(
        kernel,
        out_shape=jax.ShapeDtypeStruct((512, 128), BF16),
        in_specs=[anywhere, anywhere, vmem] + [anywhere] * 6,
        out_specs=vmem,
        scratch_shapes=[
            pltpu.VMEM((512, 1024), BF16),
            pltpu.VMEM((3, 1024, 1024), BF16),
            pltpu.VMEM((2, 1024, 128), F32),
            pltpu.VMEM((512, 128), BF16),
            pltpu.VMEM((256, 256), BF16),
            pltpu.VMEM((256, 256), BF16),
            pltpu.VMEM((128, 512), BF16),
            pltpu.VMEM((2, 256, 128), F32),
            pltpu.VMEM((UNITS, 256, 256), BF16),
            pltpu.VMEM((UNITS, 256, 256), BF16),
            pltpu.VMEM((UNITS, 2, 256, 256), BF16),
            pltpu.VMEM((UNITS, 2, 256, 256), BF16),
            pltpu.VMEM((3, 256, 256), BF16),
            pltpu.VMEM((3, 256, 256), BF16),
            pltpu.VMEM((2, 2, 128, 256), F32),
            pltpu.VMEM((512, 128), F32),
            pltpu.VMEM((512, 128), F32),
            pltpu.VMEM((2048, 128), F32),
            pltpu.VMEM((32, 64, 128), BF16),
            pltpu.VMEM((32, 64, 128), BF16),
            pltpu.VMEM((512, 128), F32),
            pltpu.VMEM((32, 16, 128), BF16),
            pltpu.VMEM((32, 16, 128), BF16),
            pltpu.VMEM((32, 16, 128), BF16),
            pltpu.VMEM((32, 16, 128), BF16),
            pltpu.SemaphoreType.DMA((10,)),
            pltpu.SemaphoreType.DMA((UNITS, 2)),
            pltpu.SemaphoreType.DMA((UNITS, 2)),
            pltpu.SemaphoreType.DMA((UNITS, 4)),
            pltpu.SemaphoreType.DMA((UNITS, 4)),
            pltpu.SemaphoreType.DMA((3,)),
            pltpu.SemaphoreType.DMA((3,)),
            pltpu.SemaphoreType.DMA((3,)),
            pltpu.SemaphoreType.DMA((3,)),
            pltpu.SemaphoreType.REGULAR,
        ],
        compiler_params=pltpu.CompilerParams(
            collective_id=0, has_side_effects=True, vmem_limit_bytes=60 * 1024 * 1024
        ),
        cost_estimate=pl.CostEstimate(flops=4_000_000_000, bytes_accessed=9_000_000, transcendentals=0),
    )(tokens, jnp.transpose(in_weight, (1, 0, 2)), skip_gain.reshape(1, 128), response.reshape(2, 1024, 128),
      first, second, back, last, twist)


def solution(mesh):
    in_specs = (P("ctx", "tp"), P("tp", None, None), P("tp"), P(None, None, "ctx", "tp"))
    return jax.shard_map(
        per_device, mesh=mesh, in_specs=in_specs, out_specs=P("ctx", "tp"), check_vma=False
    )
```
